512 devices in a mesh: level: 16 (over x_lo, y), seq: 32 (over z, x_hi, core).
Axes of the slice: x: 4 (x_hi: 2, x_lo: 2; x = x_hi * 2 + x_lo), y: 8, z: 8, core: 2. Of those that a mesh axis runs over, the one named last changes fastest.
Arguments:
- queries: bfloat16 [16, 8192, 1536], P('level', 'seq'), may hold values from -9 to 9
- keys: bfloat16 [16, 8192, 1536], P('level', 'seq'), may hold values from -9 to 9
- values: bfloat16 [16, 8192, 1536], P('level', 'seq'), may hold values from -6 to 6
- state: bfloat16 [16, 8192, 1536], P('level', 'seq'), may hold values from -6 to 6
- timestep: int32 [16], P('level'), may hold values from 1 to 16
- gate_table: bfloat16 [16, 1536], replicated, may hold values from -4 to 4
Outputs:
- velocity: bfloat16 [16, 8192, 1536], P('level', 'seq')
- advanced: bfloat16 [16, 8192, 1536], P('level', 'seq')
The draws below stay inside these ranges and needn't reach their ends.
All inputs are finite; a program needn't handle non-finite values.
Results may differ from the reference program's by a relative error of at most 0.0051.
Values may be sent and summed in bfloat16 or wider, within the bound.
A program may use at most 64 MiB of HBM per device.

```python
import math
import jax
import jax.numpy as jnp
from jax import lax

HEADS = 12
HEAD_DIM = 128
REACH = 2
STEPS = 16
TOK_DEV = 256
TOKENS = 8192
N_LEVEL = 16
N_SEQ = 32


def draw_queries(key, part):
    key = jax.random.fold_in(key, 11)
    full_shape = (N_LEVEL, TOKENS, HEADS * HEAD_DIM)
    return jnp.clip(1.5 * jax.random.normal(key, full_shape, jnp.float32), -9.0, 9.0).astype(jnp.bfloat16)


def draw_keys(key, part):
    key = jax.random.fold_in(key, 12)
    full_shape = (N_LEVEL, TOKENS, HEADS * HEAD_DIM)
    return jnp.clip(1.5 * jax.random.normal(key, full_shape, jnp.float32), -9.0, 9.0).astype(jnp.bfloat16)


def plant(drawn, stream_key, low, largest):
    longest = drawn.shape.index(max(drawn.shape))
    spots = []
    for shift in (0, 1):
        where = [jax.random.randint(jax.random.fold_in(stream_key, axis), (), 0, length) for axis, length in enumerate(drawn.shape)]
        where[longest] = (where[longest] + shift) % drawn.shape[longest]
        spots.append(tuple(where))
    return drawn.at[spots[0]].set(low).at[spots[1]].set(largest)


def level_of(rng, shape, pieces, low, largest):
    def one(axis_at, shards_of):
        heights = jax.random.uniform(jax.random.fold_in(jax.random.fold_in(rng, 6), axis_at), (shards_of,), jnp.float32, low / len(pieces), largest / len(pieces))
        return jnp.repeat(jnp.exp(heights), shape[axis_at] // shards_of).reshape((-1,) + (1,) * (len(shape) - axis_at - 1))

    loudness = one(*pieces[0])
    for cut in pieces[1:]:
        loudness = loudness * one(*cut)
    return loudness


def bell_draw(own_key, dims, width, limit, split=(), kind=jnp.bfloat16):
    values = jax.random.normal(own_key, dims, jnp.float32) * width
    if len(split) > 0:
        values = level_of(own_key, dims, split, -0.22, 0.18) * values
    return jnp.clip(values, min=-limit, max=limit).astype(kind)


def setup_inputs(seed: int = 0) -> dict:
    key_of = jax.random.split(jax.random.key(seed), 7)
    return {
        "queries": draw_queries(jax.random.fold_in(key_of[6], 71), 0),
        "keys": draw_keys(jax.random.fold_in(key_of[6], 71), 0),
        "values": bell_draw(key_of[2], (N_LEVEL, TOKENS, HEADS * HEAD_DIM), 1.0, 6.0, ((0, 16), (1, 32))),
        "state": bell_draw(key_of[3], (N_LEVEL, TOKENS, HEADS * HEAD_DIM), 1.0, 6.0, ((0, 16), (1, 32))),
        "timestep": plant(jax.random.randint(key_of[4], (N_LEVEL,), 1, STEPS + 1), jax.random.fold_in(key_of[4], 1), 1, STEPS).astype(jnp.int32),
        "gate_table": bell_draw(key_of[5], (STEPS, HEADS * HEAD_DIM), 1.0, 4.0),
    }


PAIRED = 2
FLOOR_VALUE = -1e+30

def block_parts(query_rows, key_blocks, value_blocks):
    query_count = query_rows.shape[0]
    block_count = key_blocks.shape[0]
    block_width = key_blocks.shape[1]
    group_count = HEADS // PAIRED
    query_groups = jnp.moveaxis(query_rows.reshape(query_count, group_count, PAIRED, HEAD_DIM), 1, 0)
    key_groups = jnp.moveaxis(key_blocks.reshape(block_count, block_width, group_count, PAIRED, HEAD_DIM), 2, 0)
    value_groups = jnp.moveaxis(value_blocks.reshape(block_count, block_width, group_count, PAIRED, HEAD_DIM), 2, 0)
    scaling = 1.0 / math.sqrt(HEAD_DIM)

    def one_group(operands):
        query_part, key_part, value_part = operands
        scores = jnp.einsum('qhe,cshe->chqs', query_part.astype(jnp.float32), key_part.astype(jnp.float32)) * scaling
        highest = lax.optimization_barrier(jnp.max(scores, axis=-1))
        weights = jnp.exp(scores - highest[..., None])
        totals = lax.optimization_barrier(jnp.sum(weights, axis=-1))
        rounded = lax.optimization_barrier(weights.astype(jnp.bfloat16)).astype(jnp.float32)
        blended = jnp.einsum('chqs,cshe->cqhe', rounded, value_part.astype(jnp.float32))
        partial_out = (blended / jnp.moveaxis(totals, 1, 2)[..., None]).astype(jnp.bfloat16)
        return (partial_out, highest + jnp.log(totals))
    partial_out, log_totals = lax.map(one_group, (query_groups, key_groups, value_groups))
    partial_out = jnp.moveaxis(partial_out, 0, 2).reshape(block_count, query_count, HEADS * HEAD_DIM)
    log_totals = jnp.moveaxis(log_totals, 0, 1).reshape(block_count, HEADS, query_count)
    return (partial_out, log_totals)

def merge_parts(partial_out, log_totals, usable):
    masked = jnp.where(usable[:, None, None], log_totals, FLOOR_VALUE)
    highest = lax.optimization_barrier(jnp.max(masked, axis=0))
    weights = jnp.exp(masked - highest[None])
    totals = lax.optimization_barrier(jnp.sum(weights, axis=0))
    block_count = partial_out.shape[0]
    query_count = partial_out.shape[1]
    split_out = partial_out.reshape(block_count, query_count, HEADS, HEAD_DIM).astype(jnp.float32)
    summed = jnp.einsum('cqhe,chq->qhe', split_out, weights)
    return (summed / jnp.moveaxis(totals, 0, 1)[..., None]).reshape(query_count, HEADS * HEAD_DIM)

def reference(queries, keys, values, state, timestep, gate_table):
    window = 2 * REACH + 1
    feature_width = HEADS * HEAD_DIM

    def one_level(operands):
        query_level, key_level, value_level, state_level, step_index = operands
        pad_rows = ((REACH * TOK_DEV, REACH * TOK_DEV), (0, 0))
        key_padded = jnp.pad(key_level, pad_rows)
        value_padded = jnp.pad(value_level, pad_rows)

        def one_block(block_index):
            query_rows = lax.dynamic_slice_in_dim(query_level, block_index * TOK_DEV, TOK_DEV, 0)
            key_rows = lax.dynamic_slice_in_dim(key_padded, block_index * TOK_DEV, window * TOK_DEV, 0)
            value_rows = lax.dynamic_slice_in_dim(value_padded, block_index * TOK_DEV, window * TOK_DEV, 0)
            partial_out, log_totals = block_parts(query_rows, key_rows.reshape(window, TOK_DEV, feature_width), value_rows.reshape(window, TOK_DEV, feature_width))
            nearby = block_index + jnp.arange(window, dtype=jnp.int32) - REACH
            usable = (nearby >= 0) & (nearby < N_SEQ)
            return merge_parts(partial_out, log_totals, usable)
        attended = lax.map(one_block, jnp.arange(N_SEQ, dtype=jnp.int32)).reshape(TOKENS, feature_width)
        gate_row = gate_table[step_index - 1].astype(jnp.float32)
        velocity = (gate_row[None, :] * attended).astype(jnp.bfloat16)
        factor = -(2.0 * step_index.astype(jnp.float32) - 1.0) / (STEPS * STEPS)
        updated = (state_level.astype(jnp.float32) + factor * velocity.astype(jnp.float32)).astype(jnp.bfloat16)
        return (velocity, updated)
    velocity, updated = lax.map(one_level, (queries, keys, values, state, timestep))
    return (velocity, jnp.roll(updated, -1, axis=0))
```

```python
import math

import jax
import jax.numpy as jnp
from jax import lax
from jax.experimental import pallas as pl
from jax.experimental.pallas import tpu as pltpu
from jax.sharding import PartitionSpec as P

HEADS = 12
HEAD_DIM = 128
STEPS = 16
TOK = 256
N_LEVEL = 16
N_Y = 8
N_Z = 8
WINDOW = 3
LAG_PASS = 2
LAG_COMPUTE = 3
MESH = pl.DeviceIdType.MESH
OWN, SIB, ACROSS, ALONG, SHARED = range(5)
FLOOR_VALUE = -1e30


def columns(ref, head):
    return ref.at[:, pl.ds(pl.multiple_of(head * HEAD_DIM, HEAD_DIM), HEAD_DIM)]


def kernel(
    ts_ref, gate_ref, q_hbm, k_hbm, v_hbm, s_hbm, vel_hbm, adv_hbm,
    kv, qs, ss, vel, upd, gates,
    sem_k, sem_v, sem_q, sem_s, sem_vel,
    send_sib, recv_sib, send_x, recv_x, send_z, recv_z, send_d, recv_d, send_l, recv_l,
):
    level = lax.axis_index("level")
    seq = lax.axis_index("seq")
    core = seq % 2
    x_hi = (seq // 2) % 2
    z = seq // 4

    def at(z_, x_hi_, core_):
        return (level, z_ * 4 + x_hi_ * 2 + core_)

    sibling = at(z, x_hi, 1 - core)
    across = at(z, 1 - x_hi, core)
    along_to = at((z + 1 + (N_Z - 2) * x_hi) % N_Z, x_hi, core)
    along_from = at((z + N_Z - 1 - (N_Z - 2) * x_hi) % N_Z, x_hi, core)
    level_to = ((level + N_LEVEL - 1) % N_LEVEL, seq)
    level_from = ((level + 1) % N_LEVEL, seq)

    def load_k(h):
        return pltpu.make_async_copy(columns(k_hbm, h), kv.at[OWN, h, 0], sem_k.at[h])

    def load_v(h):
        return pltpu.make_async_copy(columns(v_hbm, h), kv.at[OWN, h, 1], sem_v.at[h])

    def load_q(h):
        return pltpu.make_async_copy(columns(q_hbm, h), qs.at[h], sem_q.at[h])

    def load_s(h):
        return pltpu.make_async_copy(columns(s_hbm, h), ss.at[h], sem_s.at[h])

    def store_vel(h):
        return pltpu.make_async_copy(vel.at[h], columns(vel_hbm, h), sem_vel.at[h])

    def remote(source, target, send, recv, h, device):
        return pltpu.make_async_remote_copy(
            source, target, send.at[h], recv.at[h], device_id=device, device_id_type=MESH
        )

    def to_sibling(h):
        return remote(kv.at[OWN, h], kv.at[SIB, h], send_sib, recv_sib, h, sibling)

    def to_across(h):
        return remote(kv.at[OWN, h], kv.at[ACROSS, h], send_x, recv_x, h, across)

    def to_along(h):
        return remote(kv.at[ACROSS, h], kv.at[ALONG, h], send_z, recv_z, h, along_to)

    def share_across(h):
        return remote(kv.at[ACROSS, h], kv.at[SHARED, h], send_d, recv_d, h, sibling)

    def share_along(h):
        return remote(kv.at[ALONG, h], kv.at[SHARED, h], send_d, recv_d, h, sibling)

    def to_level(h):
        return remote(upd.at[h], columns(adv_hbm, h), send_l, recv_l, h, level_to)

    for h in range(HEADS):
        load_k(h).start()
        load_v(h).start()
    for h in range(HEADS):
        load_q(h).start()
        load_s(h).start()

    barrier = pltpu.get_barrier_semaphore()
    for device in (sibling, across, along_from, level_from):
        pl.semaphore_signal(barrier, inc=1, device_id=device, device_id_type=MESH)

    step_index = ts_ref[0]
    chosen = lax.broadcasted_iota(jnp.int32, (STEPS, HEADS * HEAD_DIM), 0) == step_index - 1
    gate_row = jnp.sum(
        jnp.where(chosen, gate_ref[...].astype(jnp.float32), 0.0), axis=0, keepdims=True
    )
    for h in range(HEADS):
        gates[h] = jnp.broadcast_to(gate_row[:, h * HEAD_DIM : (h + 1) * HEAD_DIM], (8, HEAD_DIM))
    factor = -(2.0 * step_index.astype(jnp.float32) - 1.0) / (STEPS * STEPS)

    pl.semaphore_wait(barrier, 4)

    def send_own(h):
        load_k(h).wait()
        load_v(h).wait()
        to_across(h).start()
        to_sibling(h).start()

    for h in range(WINDOW):
        send_own(h)

    end = ((z == 0) & (x_hi == 0)) | ((z == N_Z - 1) & (x_hi == 1))
    shares_across = core == x_hi
    bias_along = jnp.where(end, FLOOR_VALUE, 0.0)
    bias_shared = jnp.where(end & shares_across, FLOOR_VALUE, 0.0)
    scaling = math.log2(math.e) / math.sqrt(HEAD_DIM)

    def compute(h):
        load_q(h).wait()
        load_s(h).wait()
        query = qs[h]
        scores = []
        for slot in range(5):
            part = (
                lax.dot_general(
                    query, kv[slot, h, 0], (((1,), (1,)), ((), ())),
                    preferred_element_type=jnp.float32,
                )
                * scaling
            )
            if slot == ALONG:
                part = part + bias_along
            if slot == SHARED:
                part = part + bias_shared
            scores.append(part)
        top = scores[0]
        for part in scores[1:]:
            top = jnp.maximum(top, part)
        top = jnp.max(top, axis=-1, keepdims=True)
        total = None
        blended = None
        for slot in range(5):
            weights = jnp.exp2(scores[slot] - top)
            total = weights if total is None else total + weights
            product = jnp.dot(
                weights.astype(jnp.bfloat16), kv[slot, h, 1], preferred_element_type=jnp.float32
            )
            blended = product if blended is None else blended + product
        attended = blended / jnp.sum(total, axis=-1, keepdims=True)
        velocity = (gates[h][0:1] * attended).astype(jnp.bfloat16)
        vel[h] = velocity
        upd[h] = (ss[h].astype(jnp.float32) + factor * velocity.astype(jnp.float32)).astype(
            jnp.bfloat16
        )
        store_vel(h).start()
        to_level(h).start()

    def step(t, carry):
        @pl.when(t < HEADS)
        def _():
            to_across(t).wait_recv()
            to_along(t).start()

            @pl.when(shares_across)
            def _():
                share_across(t).start()

            @pl.when(t + WINDOW < HEADS)
            def _():
                send_own(t + WINDOW)

        @pl.when((t >= LAG_PASS) & (t < LAG_PASS + HEADS))
        def _():
            to_along(t - LAG_PASS).wait_recv()

            @pl.when(jnp.logical_not(shares_across))
            def _():
                share_along(t - LAG_PASS).start()

        @pl.when(t >= LAG_COMPUTE)
        def _():
            h = t - LAG_COMPUTE
            to_sibling(h).wait_recv()
            share_across(h).wait_recv()
            compute(h)

        return carry

    lax.fori_loop(0, HEADS + LAG_COMPUTE, step, 0)

    def drain(h, carry):
        to_sibling(h).wait_send()
        to_across(h).wait_send()
        to_along(h).wait_send()
        share_across(h).wait_send()
        store_vel(h).wait()
        to_level(h).wait_send()
        to_level(h).wait_recv()
        return carry

    lax.fori_loop(0, HEADS, drain, 0)


def on_device(queries, keys, values, state, timestep, gate_table):
    width = HEADS * HEAD_DIM
    anywhere = pl.BlockSpec(memory_space=pltpu.HBM)
    block = jax.ShapeDtypeStruct((TOK, width), jnp.bfloat16)
    heads = (HEADS, TOK, HEAD_DIM)
    velocity, advanced = pl.pallas_call(
        kernel,
        out_shape=(block, block),
        in_specs=[
            pl.BlockSpec(memory_space=pltpu.SMEM),
            pl.BlockSpec(memory_space=pltpu.VMEM),
            anywhere, anywhere, anywhere, anywhere,
        ],
        out_specs=(anywhere, anywhere),
        scratch_shapes=[
            pltpu.VMEM((5, HEADS, 2, TOK, HEAD_DIM), jnp.bfloat16),
            pltpu.VMEM(heads, jnp.bfloat16),
            pltpu.VMEM(heads, jnp.bfloat16),
            pltpu.VMEM(heads, jnp.bfloat16),
            pltpu.VMEM(heads, jnp.bfloat16),
            pltpu.VMEM((HEADS, 8, HEAD_DIM), jnp.float32),
        ]
        + [pltpu.SemaphoreType.DMA((HEADS,))] * 15,
        compiler_params=pltpu.CompilerParams(
            collective_id=0, has_side_effects=True, vmem_limit_bytes=60 << 20
        ),
        name="window_attention",
    )(timestep, gate_table, queries[0], keys[0], values[0], state[0])
    return (velocity[None], advanced[None])


def solution(mesh):
    placed = (
        P("level", "seq", None),
        P("level", "seq", None),
        P("level", "seq", None),
        P("level", "seq", None),
        P("level"),
        P(),
    )
    return jax.shard_map(
        on_device,
        mesh=mesh,
        in_specs=placed,
        out_specs=(P("level", "seq", None), P("level", "seq", None)),
        check_vma=False,
    )
```

```python
import math

import jax
import jax.numpy as jnp
from jax import lax
from jax.experimental import pallas as pl
from jax.experimental.pallas import tpu as pltpu
from jax.sharding import PartitionSpec as P

HEADS = 12
HEAD_DIM = 128
STEPS = 16
TOK = 256
N_LEVEL = 16
N_Y = 8
N_Z = 8
WINDOW = 3
LAG_COMPUTE = 2
LAG_RELAY = 3
RELAYED = N_Y - 1
MESH = pl.DeviceIdType.MESH
OWN, SIB, ACROSS, ALONG, SHARED = range(5)
FLOOR_VALUE = -1e30


def columns(ref, head):
    return ref.at[:, pl.ds(pl.multiple_of(head * HEAD_DIM, HEAD_DIM), HEAD_DIM)]


def kernel(
    ts_ref, gate_hbm, q_hbm, k_hbm, v_hbm, s_hbm, vel_hbm, adv_hbm,
    kv, qs, ss, vel, upd, gate_table, gates, relay,
    sem_own, send_sib, recv_sib, send_x, recv_x, send_z, recv_z, send_d, recv_d,
    sem_q, sem_s, sem_vel, send_l, recv_l, sem_gate, send_r, recv_r,
):
    level = lax.axis_index("level")
    seq = lax.axis_index("seq")
    core = seq % 2
    x_hi = (seq // 2) % 2
    z = seq // 4
    x_lo = level // N_Y
    y = level % N_Y

    def at(z_, x_hi_, core_):
        return (level, z_ * 4 + x_hi_ * 2 + core_)

    def on_level(x_lo_, y_):
        return (x_lo_ * N_Y + y_, seq)

    sibling = at(z, x_hi, 1 - core)
    across = at(z, 1 - x_hi, core)
    along_to = at((z + 1 + (N_Z - 2) * x_hi) % N_Z, x_hi, core)
    along_from = at((z + N_Z - 1 - (N_Z - 2) * x_hi) % N_Z, x_hi, core)
    level_to = ((level + N_LEVEL - 1) % N_LEVEL, seq)
    end = ((z == 0) & (x_hi == 0)) | ((z == N_Z - 1) & (x_hi == 1))
    passes = jnp.logical_not(((z == 0) & (x_hi == 1)) | ((z == N_Z - 1) & (x_hi == 0)))
    shares_across = core == x_hi

    barrier = pltpu.get_barrier_semaphore()

    def greet(device):
        pl.semaphore_signal(barrier, inc=1, device_id=device, device_id_type=MESH)

    greet(across)
    greet(sibling)

    @pl.when(jnp.logical_not(end))
    def _():
        greet(along_from)

    greet(on_level(1 - x_lo, 0))

    @pl.when(y < RELAYED)
    def _():
        greet(on_level(x_lo, y + 1))

    @pl.when(y == RELAYED)
    def _():
        for row in range(RELAYED):
            greet(on_level(x_lo, row))

    def load_gate():
        return pltpu.make_async_copy(gate_hbm, gate_table, sem_gate)

    def own_part(h, kind):
        return columns(v_hbm if kind else k_hbm, h)

    def load_own(h, kind):
        u = 2 * h + kind
        return pltpu.make_async_copy(own_part(h, kind), kv.at[OWN, u], sem_own.at[u])

    def load_q(h):
        return pltpu.make_async_copy(columns(q_hbm, h), qs.at[h], sem_q.at[h])

    def load_s(h):
        return pltpu.make_async_copy(columns(s_hbm, h), ss.at[h], sem_s.at[h])

    def store_vel(h):
        return pltpu.make_async_copy(vel.at[h], columns(vel_hbm, h), sem_vel.at[h])

    def remote(source, target, send, recv, device):
        return pltpu.make_async_remote_copy(
            source, target, send, recv, device_id=device, device_id_type=MESH
        )

    def to_sibling(h, kind):
        u = 2 * h + kind
        return remote(kv.at[OWN, u], kv.at[SIB, u], send_sib.at[u], recv_sib.at[u], sibling)

    def to_across(h, kind):
        u = 2 * h + kind
        return remote(kv.at[OWN, u], kv.at[ACROSS, u], send_x.at[u], recv_x.at[u], across)

    def to_along(u):
        return remote(kv.at[ACROSS, u], kv.at[ALONG, u], send_z.at[u], recv_z.at[u], along_to)

    def own_as_along(u):
        return pltpu.make_async_copy(kv.at[OWN, u], kv.at[ALONG, u], recv_z.at[u])

    def share(slot, u):
        return remote(kv.at[slot, u], kv.at[SHARED, u], send_d.at[u], recv_d.at[u], sibling)

    def to_level(h):
        return remote(upd.at[h], columns(adv_hbm, h), send_l.at[h], recv_l.at[h], level_to)

    def to_relay(h):
        return remote(upd.at[h], relay, send_l.at[h], recv_r, on_level(1 - x_lo, h))

    def from_relay():
        return remote(relay, columns(adv_hbm, y), send_r, recv_l.at[y], on_level(x_lo, RELAYED))

    def send_own(h):
        for kind in range(2):
            load_own(h, kind).wait()
        for kind in range(2):
            to_across(h, kind).start()
        for kind in range(2):
            to_sibling(h, kind).start()

    def load_rest(h):
        load_q(h).start()
        load_s(h).start()

    for h in range(HEADS):
        for kind in range(2):
            load_own(h, kind).start()
    load_gate().start()
    count = 2 + passes.astype(jnp.int32) + 1 + (y < RELAYED).astype(jnp.int32)
    count = count + RELAYED * (y == 0).astype(jnp.int32)
    pl.semaphore_wait(barrier, count)
    for h in range(WINDOW):
        send_own(h)
    for h in range(WINDOW):
        load_rest(h)

    load_gate().wait()
    step_index = ts_ref[0]
    chosen = lax.broadcasted_iota(jnp.int32, (STEPS, HEADS * HEAD_DIM), 0) == step_index - 1
    gate_row = jnp.sum(
        jnp.where(chosen, gate_table[...].astype(jnp.float32), 0.0), axis=0, keepdims=True
    )
    for h in range(HEADS):
        gates[h] = jnp.broadcast_to(gate_row[:, h * HEAD_DIM : (h + 1) * HEAD_DIM], (8, HEAD_DIM))
    factor = -(2.0 * step_index.astype(jnp.float32) - 1.0) / (STEPS * STEPS)

    bias_along = jnp.where(end, FLOOR_VALUE, 0.0)
    bias_shared = jnp.where(end & shares_across, FLOOR_VALUE, 0.0)
    scaling = math.log2(math.e) / math.sqrt(HEAD_DIM)

    def compute(h):
        query = qs[h]
        scores = []
        for slot in range(5):
            part = (
                lax.dot_general(
                    query, kv[slot, 2 * h], (((1,), (1,)), ((), ())),
                    preferred_element_type=jnp.float32,
                )
                * scaling
            )
            if slot == ALONG:
                part = part + bias_along
            if slot == SHARED:
                part = part + bias_shared
            scores.append(part)
        top = scores[0]
        for part in scores[1:]:
            top = jnp.maximum(top, part)
        top = jnp.max(top, axis=-1, keepdims=True)
        total = None
        blended = None
        for slot in range(5):
            weights = jnp.exp2(scores[slot] - top)
            total = weights if total is None else total + weights
            product = jnp.dot(
                weights.astype(jnp.bfloat16), kv[slot, 2 * h + 1],
                preferred_element_type=jnp.float32,
            )
            blended = product if blended is None else blended + product
        attended = blended / jnp.sum(total, axis=-1, keepdims=True)
        velocity = (gates[h][0:1] * attended).astype(jnp.bfloat16)
        vel[h] = velocity
        upd[h] = (ss[h].astype(jnp.float32) + factor * velocity.astype(jnp.float32)).astype(
            jnp.bfloat16
        )

    def step(t, carry):
        for kind in range(2):

            @pl.when(t < HEADS)
            def _():
                u = 2 * t + kind
                to_across(t, kind).wait_recv()

                @pl.when(passes)
                def _():
                    to_along(u).start()

                @pl.when(shares_across)
                def _():
                    share(ACROSS, u).start()

            @pl.when((t >= 1) & (t <= HEADS))
            def _():
                u = 2 * t - 2 + kind

                @pl.when(end)
                def _():
                    own_as_along(u).start()

                to_along(u).wait_recv()

                @pl.when(jnp.logical_not(shares_across))
                def _():
                    share(ALONG, u).start()

        @pl.when(t + WINDOW < HEADS)
        def _():
            send_own(t + WINDOW)
            load_rest(t + WINDOW)

        @pl.when(t >= LAG_COMPUTE)
        def _():
            h = t - LAG_COMPUTE
            for kind in range(2):
                to_sibling(h, kind).wait_recv()
                share(ACROSS, 2 * h + kind).wait_recv()
            load_q(h).wait()
            load_s(h).wait()
            compute(h)

            @pl.when((y == 0) & (h < RELAYED))
            def _():
                to_relay(h).start()

            @pl.when((y > 0) | (h >= RELAYED))
            def _():
                to_level(h).start()

            store_vel(h).start()

        @pl.when((y < RELAYED) & (t == y + LAG_COMPUTE + LAG_RELAY))
        def _():
            to_relay(y).wait_recv()
            from_relay().start()

        return carry

    lax.fori_loop(0, HEADS + LAG_COMPUTE, step, 0)

    def drain(h, carry):
        for kind in range(2):
            u = 2 * h + kind
            to_sibling(h, kind).wait_send()
            to_across(h, kind).wait_send()

            @pl.when(passes)
            def _():
                to_along(u).wait_send()

            share(ACROSS, u).wait_send()
        store_vel(h).wait()
        to_level(h).wait_send()
        to_level(h).wait_recv()
        return carry

    lax.fori_loop(0, HEADS, drain, 0)

    @pl.when(y < RELAYED)
    def _():
        from_relay().wait_send()


def on_device(queries, keys, values, state, timestep, gate_table):
    width = HEADS * HEAD_DIM
    anywhere = pl.BlockSpec(memory_space=pltpu.HBM)
    block = jax.ShapeDtypeStruct((TOK, width), jnp.bfloat16)
    heads = (HEADS, TOK, HEAD_DIM)
    velocity, advanced = pl.pallas_call(
        kernel,
        out_shape=(block, block),
        in_specs=[
            pl.BlockSpec(memory_space=pltpu.SMEM),
            anywhere, anywhere, anywhere, anywhere, anywhere,
        ],
        out_specs=(anywhere, anywhere),
        scratch_shapes=[
            pltpu.VMEM((5, 2 * HEADS, TOK, HEAD_DIM), jnp.bfloat16),
            pltpu.VMEM(heads, jnp.bfloat16),
            pltpu.VMEM(heads, jnp.bfloat16),
            pltpu.VMEM(heads, jnp.bfloat16),
            pltpu.VMEM(heads, jnp.bfloat16),
            pltpu.VMEM((STEPS, width), jnp.bfloat16),
            pltpu.VMEM((HEADS, 8, HEAD_DIM), jnp.float32),
            pltpu.VMEM((TOK, HEAD_DIM), jnp.bfloat16),
        ]
        + [pltpu.SemaphoreType.DMA((2 * HEADS,))] * 9
        + [pltpu.SemaphoreType.DMA((HEADS,))] * 5
        + [pltpu.SemaphoreType.DMA] * 3,
        compiler_params=pltpu.CompilerParams(
            collective_id=0, has_side_effects=True, vmem_limit_bytes=60 << 20
        ),
        name="window_attention",
    )(timestep, gate_table, queries[0], keys[0], values[0], state[0])
    return (velocity[None], advanced[None])


def solution(mesh):
    placed = (
        P("level", "seq", None),
        P("level", "seq", None),
        P("level", "seq", None),
        P("level", "seq", None),
        P("level"),
        P(),
    )
    return jax.shard_map(
        on_device,
        mesh=mesh,
        in_specs=placed,
        out_specs=(P("level", "seq", None), P("level", "seq", None)),
        check_vma=False,
    )
```

```python
import math

import jax
import jax.numpy as jnp
from jax import lax
from jax.experimental import pallas as pl
from jax.experimental.pallas import tpu as pltpu
from jax.sharding import PartitionSpec as P

HEADS = 12
HEAD_DIM = 128
STEPS = 16
TOK = 256
N_LEVEL = 16
N_Y = 8
N_Z = 8
WINDOW = 3
PIECES = 2
LAG_PASS = 2
LAG_COMPUTE = 2
LAG_RELAY = 3
RELAYED = N_Y - 1
MESH = pl.DeviceIdType.MESH
OWN, SIB, ACROSS, ALONG, SHARED = range(5)
FLOOR_VALUE = -1e30


def columns(ref, head):
    return ref.at[:, pl.ds(pl.multiple_of(head * HEAD_DIM, HEAD_DIM), HEAD_DIM)]


def kernel(
    ts_ref, gate_hbm, q_hbm, k_hbm, v_hbm, s_hbm, vel_hbm, adv_hbm,
    kv, qs, ss, vel, upd, gate_table, gates, relay,
    sem_own, send_sib, recv_sib, send_x, recv_x, send_z, recv_z, send_d, recv_d,
    sem_q, sem_s, sem_vel, send_l, recv_l, sem_gate, send_r, recv_r, along_ready, level_ready,
):
    level = lax.axis_index("level")
    seq = lax.axis_index("seq")
    core = seq % 2
    x_hi = (seq // 2) % 2
    z = seq // 4
    x_lo = level // N_Y
    y = level % N_Y

    def at(z_, x_hi_, core_):
        return (level, z_ * 4 + x_hi_ * 2 + core_)

    def on_level(x_lo_, y_):
        return (x_lo_ * N_Y + y_, seq)

    sibling = at(z, x_hi, 1 - core)
    across = at(z, 1 - x_hi, core)
    along_to = at((z + 1 + (N_Z - 2) * x_hi) % N_Z, x_hi, core)
    level_to = ((level + N_LEVEL - 1) % N_LEVEL, seq)
    end = ((z == 0) & (x_hi == 0)) | ((z == N_Z - 1) & (x_hi == 1))
    passes = jnp.logical_not(((z == 0) & (x_hi == 1)) | ((z == N_Z - 1) & (x_hi == 0)))
    shares_across = core == x_hi

    barrier = pltpu.get_barrier_semaphore()

    def greet(device):
        pl.semaphore_signal(barrier, inc=1, device_id=device, device_id_type=MESH)

    greet(across)
    greet(sibling)

    @pl.when(z < N_Z - 1)
    def _():
        greet(at(z + 1, x_hi, core))

    @pl.when(y < N_Y - 1)
    def _():
        greet(on_level(x_lo, y + 1))

    @pl.when(y == 0)
    def _():
        for row in range(N_Y):
            greet(on_level(1 - x_lo, row))

    def load_gate():
        return pltpu.make_async_copy(gate_hbm, gate_table, sem_gate)

    def own_part(h, kind):
        return columns(v_hbm if kind else k_hbm, h)

    def load_own(h, kind):
        u = 2 * h + kind
        return pltpu.make_async_copy(own_part(h, kind), kv.at[OWN, u], sem_own.at[u])

    def load_q(h):
        return pltpu.make_async_copy(columns(q_hbm, h), qs.at[h], sem_q.at[h])

    def load_s(h):
        return pltpu.make_async_copy(columns(s_hbm, h), ss.at[h], sem_s.at[h])

    def store_vel(h):
        return pltpu.make_async_copy(vel.at[h], columns(vel_hbm, h), sem_vel.at[h])

    def remote(source, target, send, recv, device):
        return pltpu.make_async_remote_copy(
            source, target, send, recv, device_id=device, device_id_type=MESH
        )

    def to_sibling(h, kind):
        u = 2 * h + kind
        return remote(kv.at[OWN, u], kv.at[SIB, u], send_sib.at[u], recv_sib.at[u], sibling)

    def to_across(h, kind):
        u = 2 * h + kind
        return remote(kv.at[OWN, u], kv.at[ACROSS, u], send_x.at[u], recv_x.at[u], across)

    def to_along(u):
        return remote(kv.at[ACROSS, u], kv.at[ALONG, u], send_z.at[u], recv_z.at[u], along_to)

    def own_as_along(u):
        return pltpu.make_async_copy(kv.at[OWN, u], kv.at[ALONG, u], recv_z.at[u])

    def share(slot, u):
        return remote(kv.at[slot, u], kv.at[SHARED, u], send_d.at[u], recv_d.at[u], sibling)

    def to_level(h):
        return remote(upd.at[h], columns(adv_hbm, h), send_l.at[h], recv_l.at[h], level_to)

    def to_relay(h):
        return remote(upd.at[h], relay, send_l.at[h], recv_r, on_level(1 - x_lo, h))

    def from_relay():
        return remote(relay, columns(adv_hbm, y), send_r, recv_l.at[y], on_level(x_lo, RELAYED))

    def send_own(h):
        for kind in range(2):
            load_own(h, kind).wait()
        for kind in range(2):
            to_across(h, kind).start()
        for kind in range(2):
            to_sibling(h, kind).start()

    def load_rest(h):
        load_q(h).start()
        load_s(h).start()

    for h in range(HEADS):
        for kind in range(2):
            load_own(h, kind).start()
    load_gate().start()
    pl.semaphore_wait(barrier, 3 + (z > 0).astype(jnp.int32) + (y > 0).astype(jnp.int32))
    for h in range(WINDOW):
        send_own(h)
    @pl.when((x_hi == 0) & (z > 0))
    def _():
        pl.semaphore_signal(
            along_ready, inc=1, device_id=at(z - 1, x_hi, core), device_id_type=MESH
        )

    pl.semaphore_signal(
        level_ready, inc=1, device_id=on_level(1 - x_lo, 0), device_id_type=MESH
    )
    for h in range(WINDOW):
        load_rest(h)

    load_gate().wait()
    step_index = ts_ref[0]
    chosen = lax.broadcasted_iota(jnp.int32, (STEPS, HEADS * HEAD_DIM), 0) == step_index - 1
    gate_row = jnp.sum(
        jnp.where(chosen, gate_table[...].astype(jnp.float32), 0.0), axis=0, keepdims=True
    )
    for h in range(HEADS):
        gates[h] = jnp.broadcast_to(gate_row[:, h * HEAD_DIM : (h + 1) * HEAD_DIM], (8, HEAD_DIM))
    factor = -(2.0 * step_index.astype(jnp.float32) - 1.0) / (STEPS * STEPS)

    bias_along = jnp.where(end, FLOOR_VALUE, 0.0)
    bias_shared = jnp.where(end & shares_across, FLOOR_VALUE, 0.0)
    scaling = math.log2(math.e) / math.sqrt(HEAD_DIM)

    def compute(h):
        query = qs[h]
        scores = []
        for slot in range(5):
            part = (
                lax.dot_general(
                    query, kv[slot, 2 * h], (((1,), (1,)), ((), ())),
                    preferred_element_type=jnp.float32,
                )
                * scaling
            )
            if slot == ALONG:
                part = part + bias_along
            if slot == SHARED:
                part = part + bias_shared
            scores.append(part)
        top = scores[0]
        for part in scores[1:]:
            top = jnp.maximum(top, part)
        top = jnp.max(top, axis=-1, keepdims=True)
        total = None
        blended = None
        for slot in range(5):
            weights = jnp.exp2(scores[slot] - top)
            total = weights if total is None else total + weights
            product = jnp.dot(
                weights.astype(jnp.bfloat16), kv[slot, 2 * h + 1],
                preferred_element_type=jnp.float32,
            )
            blended = product if blended is None else blended + product
        attended = blended / jnp.sum(total, axis=-1, keepdims=True)
        velocity = (gates[h][0:1] * attended).astype(jnp.bfloat16)
        vel[h] = velocity
        upd[h] = (ss[h].astype(jnp.float32) + factor * velocity.astype(jnp.float32)).astype(
            jnp.bfloat16
        )

    def step(t, carry):
        def arrived(kind):
            u = 2 * t + kind
            to_across(t, kind).wait_recv()

            @pl.when(passes)
            def _():
                to_along(u).start()

            @pl.when(shares_across)
            def _():
                share(ACROSS, u).start()

        @pl.when(t < HEADS)
        def _():
            arrived(0)

        @pl.when((t >= LAG_PASS) & (t < HEADS + LAG_PASS))
        def _():
            for kind in range(2):
                u = 2 * (t - LAG_PASS) + kind

                @pl.when(end)
                def _():
                    own_as_along(u).start()

                to_along(u).wait_recv()

                @pl.when(jnp.logical_not(shares_across))
                def _():
                    share(ALONG, u).start()

        @pl.when(t < HEADS)
        def _():
            arrived(1)

        @pl.when(t + WINDOW < HEADS)
        def _():
            send_own(t + WINDOW)
            load_rest(t + WINDOW)

        @pl.when(t >= LAG_COMPUTE)
        def _():
            h = t - LAG_COMPUTE
            for kind in range(2):
                to_sibling(h, kind).wait_recv()
                share(ACROSS, 2 * h + kind).wait_recv()
            load_q(h).wait()
            load_s(h).wait()
            compute(h)

            @pl.when((y == 0) & (h == 0))
            def _():
                pl.semaphore_wait(level_ready, N_Y)

            @pl.when((y == 0) & (h < RELAYED))
            def _():
                to_relay(h).start()

            @pl.when((y > 0) | (h >= RELAYED))
            def _():
                to_level(h).start()

            store_vel(h).start()

        @pl.when((y < RELAYED) & (t == y + LAG_COMPUTE + LAG_RELAY))
        def _():
            to_relay(y).wait_recv()
            from_relay().start()

        return carry

    @pl.when((x_hi == 0) & (z < N_Z - 1))
    def _():
        pl.semaphore_wait(along_ready, 1)

    lax.fori_loop(0, HEADS + LAG_COMPUTE, step, 0)

    def drain(h, carry):
        for kind in range(2):
            u = 2 * h + kind
            to_sibling(h, kind).wait_send()
            to_across(h, kind).wait_send()

            @pl.when(passes)
            def _():
                to_along(u).wait_send()

            share(ACROSS, u).wait_send()
        store_vel(h).wait()
        to_level(h).wait_send()
        to_level(h).wait_recv()
        return carry

    lax.fori_loop(0, HEADS, drain, 0)

    @pl.when(y < RELAYED)
    def _():
        from_relay().wait_send()


def write_out(vel_from, adv_from, vel_to, adv_to, sems):
    rows = TOK // PIECES
    moves = []
    for i, (source, target) in enumerate(((vel_from, vel_to), (adv_from, adv_to))):
        for j in range(PIECES):
            part = pl.ds(j * rows, rows)
            moves.append(pltpu.make_async_copy(source.at[part], target.at[part], sems.at[i, j]))
    for move in moves:
        move.start()
    for move in moves:
        move.wait()


def on_device(queries, keys, values, state, timestep, gate_table):
    width = HEADS * HEAD_DIM
    anywhere = pl.BlockSpec(memory_space=pltpu.HBM)
    block = jax.ShapeDtypeStruct((TOK, width), jnp.bfloat16)
    heads = (HEADS, TOK, HEAD_DIM)
    velocity, advanced = pl.pallas_call(
        kernel,
        out_shape=(block, block),
        in_specs=[
            pl.BlockSpec(memory_space=pltpu.SMEM),
            anywhere, anywhere, anywhere, anywhere, anywhere,
        ],
        out_specs=(anywhere, anywhere),
        scratch_shapes=[
            pltpu.VMEM((5, 2 * HEADS, TOK, HEAD_DIM), jnp.bfloat16),
            pltpu.VMEM(heads, jnp.bfloat16),
            pltpu.VMEM(heads, jnp.bfloat16),
            pltpu.VMEM(heads, jnp.bfloat16),
            pltpu.VMEM(heads, jnp.bfloat16),
            pltpu.VMEM((STEPS, width), jnp.bfloat16),
            pltpu.VMEM((HEADS, 8, HEAD_DIM), jnp.float32),
            pltpu.VMEM((TOK, HEAD_DIM), jnp.bfloat16),
        ]
        + [pltpu.SemaphoreType.DMA((2 * HEADS,))] * 9
        + [pltpu.SemaphoreType.DMA((HEADS,))] * 5
        + [pltpu.SemaphoreType.DMA] * 3
        + [pltpu.SemaphoreType.REGULAR] * 2,
        compiler_params=pltpu.CompilerParams(
            collective_id=0, has_side_effects=True, vmem_limit_bytes=32 << 20
        ),
        name="window_attention",
    )(timestep, *[pltpu.with_memory_space_constraint(a, pltpu.HBM) for a in (gate_table, queries[0], keys[0], values[0], state[0])])
    velocity, advanced = pl.pallas_call(
        write_out,
        out_shape=(block, block),
        in_specs=[pl.BlockSpec(memory_space=pltpu.VMEM)] * 2,
        out_specs=(anywhere, anywhere),
        scratch_shapes=[pltpu.SemaphoreType.DMA((2, PIECES))],
        compiler_params=pltpu.CompilerParams(vmem_limit_bytes=16 << 20),
        name="write_out",
    )(velocity, advanced)
    return (velocity[None], advanced[None])


def solution(mesh):
    placed = (
        P("level", "seq", None),
        P("level", "seq", None),
        P("level", "seq", None),
        P("level", "seq", None),
        P("level"),
        P(),
    )
    return jax.shard_map(
        on_device,
        mesh=mesh,
        in_specs=placed,
        out_specs=(P("level", "seq", None), P("level", "seq", None)),
        check_vma=False,
    )
```

```python
import math

import jax
import jax.numpy as jnp
from jax import lax
from jax.experimental import pallas as pl
from jax.experimental.pallas import tpu as pltpu
from jax.sharding import PartitionSpec as P

HEADS = 12
HEAD_DIM = 128
STEPS = 16
TOK = 256
N_LEVEL = 16
N_Y = 8
N_Z = 8
WINDOW = 3
PIECES = 2
LAG_PASS = 2
LAG_COMPUTE = 2
LAG_RELAY = 3
ROWS = (5, 6, 0, 1, 2, 3, 0)
SLOTS = (0, 0, 0, 0, 0, 0, 1)
RELAYED = len(ROWS)
KEPT = 4
MESH = pl.DeviceIdType.MESH
OWN, SIB, ACROSS, ALONG, SHARED = range(5)
FLOOR_VALUE = -1e30


def columns(ref, head):
    return ref.at[:, pl.ds(pl.multiple_of(head * HEAD_DIM, HEAD_DIM), HEAD_DIM)]


def kernel(
    ts_ref, gate_hbm, q_hbm, k_hbm, v_hbm, s_hbm, vel_hbm, adv_hbm,
    kv, tops, totals, sums, qs, ss, upd, vel, gate_table, gates, relay,
    sem_own, send_sib, recv_sib, send_x, recv_x, send_z, recv_z, send_d, recv_d,
    sem_q, sem_s, sem_vel, send_l, recv_l, sem_gate, send_r, recv_r, along_ready, level_ready,
):
    level = lax.axis_index("level")
    seq = lax.axis_index("seq")
    core = seq % 2
    x_hi = (seq // 2) % 2
    z = seq // 4
    x_lo = level // N_Y
    y = level % N_Y

    def at(z_, x_hi_, core_):
        return (level, z_ * 4 + x_hi_ * 2 + core_)

    def on_level(x_lo_, y_):
        return (x_lo_ * N_Y + y_, seq)

    sibling = at(z, x_hi, 1 - core)
    across = at(z, 1 - x_hi, core)
    along_to = at((z + 1 + (N_Z - 2) * x_hi) % N_Z, x_hi, core)
    level_to = ((level + N_LEVEL - 1) % N_LEVEL, seq)
    end = ((z == 0) & (x_hi == 0)) | ((z == N_Z - 1) & (x_hi == 1))
    passes = jnp.logical_not(((z == 0) & (x_hi == 1)) | ((z == N_Z - 1) & (x_hi == 0)))
    shares_across = core == x_hi

    barrier = pltpu.get_barrier_semaphore()

    def greet(device):
        pl.semaphore_signal(barrier, inc=1, device_id=device, device_id_type=MESH)

    greet(across)
    greet(sibling)

    @pl.when(z < N_Z - 1)
    def _():
        greet(at(z + 1, x_hi, core))

    @pl.when(y < N_Y - 1)
    def _():
        greet(on_level(x_lo, y + 1))

    @pl.when(y == 0)
    def _():
        for row in range(N_Y):
            greet(on_level(1 - x_lo, row))

    def load_gate():
        return pltpu.make_async_copy(gate_hbm, gate_table, sem_gate)

    def own_part(h, kind):
        return columns(v_hbm if kind else k_hbm, h)

    def load_own(h, kind):
        u = 2 * h + kind
        return pltpu.make_async_copy(own_part(h, kind), kv.at[OWN, u], sem_own.at[u])

    def load_q(h):
        return pltpu.make_async_copy(columns(q_hbm, h), qs.at[h], sem_q.at[h])

    def load_s(h):
        return pltpu.make_async_copy(columns(s_hbm, h), ss.at[h], sem_s.at[h])

    def store_vel(h):
        return pltpu.make_async_copy(vel.at[h], columns(vel_hbm, h), sem_vel.at[h])

    def remote(source, target, send, recv, device):
        return pltpu.make_async_remote_copy(
            source, target, send, recv, device_id=device, device_id_type=MESH
        )

    def to_sibling(h, kind):
        u = 2 * h + kind
        return remote(kv.at[OWN, u], kv.at[SIB, u], send_sib.at[u], recv_sib.at[u], sibling)

    def to_across(h, kind):
        u = 2 * h + kind
        return remote(kv.at[OWN, u], kv.at[ACROSS, u], send_x.at[u], recv_x.at[u], across)

    def to_along(u):
        return remote(kv.at[ACROSS, u], kv.at[ALONG, u], send_z.at[u], recv_z.at[u], along_to)

    def own_as_along(u):
        return pltpu.make_async_copy(kv.at[OWN, u], kv.at[ALONG, u], recv_z.at[u])

    def share(slot, u):
        return remote(kv.at[slot, u], kv.at[SHARED, u], send_d.at[u], recv_d.at[u], sibling)

    def to_level(h):
        return remote(upd.at[h], columns(adv_hbm, h), send_l.at[h], recv_l.at[h], level_to)

    def to_relay(h):
        return remote(
            upd.at[h], relay.at[SLOTS[h]], send_l.at[h], recv_r.at[SLOTS[h]],
            on_level(1 - x_lo, ROWS[h]),
        )

    def from_relay(h):
        return remote(
            relay.at[SLOTS[h]], columns(adv_hbm, h), send_r.at[SLOTS[h]], recv_l.at[h],
            on_level(x_lo, N_Y - 1),
        )

    def send_own(h):
        for kind in range(2):
            load_own(h, kind).wait()
        for kind in range(2):
            to_across(h, kind).start()
        for kind in range(2):
            to_sibling(h, kind).start()

    def load_rest(h):
        load_q(h).start()
        load_s(h).start()

    for h in range(HEADS):
        for kind in range(2):
            load_own(h, kind).start()
    load_gate().start()
    pl.semaphore_wait(barrier, 3 + (z > 0).astype(jnp.int32) + (y > 0).astype(jnp.int32))
    for h in range(WINDOW):
        send_own(h)
    @pl.when((x_hi == 0) & (z > 0))
    def _():
        pl.semaphore_signal(
            along_ready, inc=1, device_id=at(z - 1, x_hi, core), device_id_type=MESH
        )

    pl.semaphore_signal(
        level_ready, inc=1, device_id=on_level(1 - x_lo, 0), device_id_type=MESH
    )
    for h in range(WINDOW):
        load_rest(h)

    load_gate().wait()
    step_index = ts_ref[0]
    chosen = lax.broadcasted_iota(jnp.int32, (STEPS, HEADS * HEAD_DIM), 0) == step_index - 1
    gate_row = jnp.sum(
        jnp.where(chosen, gate_table[...].astype(jnp.float32), 0.0), axis=0, keepdims=True
    )
    for h in range(HEADS):
        gates[h] = jnp.broadcast_to(gate_row[:, h * HEAD_DIM : (h + 1) * HEAD_DIM], (8, HEAD_DIM))
    factor = -(2.0 * step_index.astype(jnp.float32) - 1.0) / (STEPS * STEPS)

    bias_along = jnp.where(end, FLOOR_VALUE, 0.0)
    bias_shared = jnp.where(end & shares_across, FLOOR_VALUE, 0.0)
    scaling = math.log2(math.e) / math.sqrt(HEAD_DIM)

    def score(h, slot):
        part = (
            lax.dot_general(
                qs[h], kv[slot, 2 * h], (((1,), (1,)), ((), ())),
                preferred_element_type=jnp.float32,
            )
            * scaling
        )
        if slot == ALONG:
            part = part + bias_along
        if slot == SHARED:
            part = part + bias_shared
        return part

    def weigh(h, slots, scores, top):
        total = None
        blended = None
        for slot, part in zip(slots, scores):
            weights = jnp.exp2(part - top)
            total = weights if total is None else total + weights
            product = jnp.dot(
                weights.astype(jnp.bfloat16), kv[slot, 2 * h + 1],
                preferred_element_type=jnp.float32,
            )
            blended = product if blended is None else blended + product
        return jnp.sum(total, axis=-1, keepdims=True), blended

    def highest(scores):
        top = scores[0]
        for part in scores[1:]:
            top = jnp.maximum(top, part)
        return jnp.max(top, axis=-1, keepdims=True)

    FIRST, REST = (OWN, SIB, ACROSS), (ALONG, SHARED)

    def compute_first(h):
        place = lax.rem(h, KEPT)
        scores = [score(h, slot) for slot in FIRST]
        top = highest(scores)
        total, blended = weigh(h, FIRST, scores, top)
        tops[place] = top
        totals[place] = total
        sums[place] = blended

    def compute_rest(h):
        place = lax.rem(h, KEPT)
        scores = [score(h, slot) for slot in REST]
        top = jnp.maximum(highest(scores), tops[place])
        total, blended = weigh(h, REST, scores, top)
        kept = jnp.exp2(tops[place] - top)
        total = total + totals[place] * kept
        attended = (blended + sums[place] * kept) / total
        velocity = (gates[h][0:1] * attended).astype(jnp.bfloat16)
        vel[h] = velocity
        upd[h] = (ss[h].astype(jnp.float32) + factor * velocity.astype(jnp.float32)).astype(
            jnp.bfloat16
        )

    def step(t, carry):
        def arrived(kind):
            u = 2 * t + kind
            to_across(t, kind).wait_recv()

            @pl.when(passes)
            def _():
                to_along(u).start()

            @pl.when(shares_across)
            def _():
                share(ACROSS, u).start()

        @pl.when(t < HEADS)
        def _():
            arrived(0)

        @pl.when((t >= LAG_PASS) & (t < HEADS + LAG_PASS))
        def _():
            for kind in range(2):
                u = 2 * (t - LAG_PASS) + kind

                @pl.when(end)
                def _():
                    own_as_along(u).start()

                to_along(u).wait_recv()

                @pl.when(jnp.logical_not(shares_across))
                def _():
                    share(ALONG, u).start()

        @pl.when(t < HEADS)
        def _():
            arrived(1)

        @pl.when(t + WINDOW < HEADS)
        def _():
            send_own(t + WINDOW)
            load_rest(t + WINDOW)

        @pl.when(t >= LAG_COMPUTE)
        def _():
            h = t - LAG_COMPUTE
            for kind in range(2):
                share(ACROSS, 2 * h + kind).wait_recv()
            load_s(h).wait()
            compute_rest(h)

            @pl.when((y == 0) & (h == 0))
            def _():
                pl.semaphore_wait(level_ready, N_Y)

            for i in range(RELAYED):

                @pl.when((y == 0) & (h == i))
                def _():
                    to_relay(i).start()

            @pl.when((y > 0) | (h >= RELAYED))
            def _():
                to_level(h).start()

            store_vel(h).start()

        @pl.when(t < HEADS)
        def _():
            for kind in range(2):
                to_sibling(t, kind).wait_recv()
            load_q(t).wait()
            compute_first(t)

        for i in range(RELAYED):

            @pl.when((y == ROWS[i]) & (t == i + LAG_COMPUTE + LAG_RELAY))
            def _():
                to_relay(i).wait_recv()
                from_relay(i).start()

        return carry

    @pl.when((x_hi == 0) & (z < N_Z - 1))
    def _():
        pl.semaphore_wait(along_ready, 1)

    lax.fori_loop(0, HEADS + LAG_COMPUTE, step, 0)

    def drain(h, carry):
        for kind in range(2):
            u = 2 * h + kind
            to_sibling(h, kind).wait_send()
            to_across(h, kind).wait_send()

            @pl.when(passes)
            def _():
                to_along(u).wait_send()

            share(ACROSS, u).wait_send()
        store_vel(h).wait()
        to_level(h).wait_send()
        to_level(h).wait_recv()
        return carry

    lax.fori_loop(0, HEADS, drain, 0)

    for i in range(RELAYED):

        @pl.when(y == ROWS[i])
        def _():
            from_relay(i).wait_send()


def write_out(vel_from, adv_from, vel_to, adv_to, sems):
    rows = TOK // PIECES
    moves = []
    for i, (source, target) in enumerate(((vel_from, vel_to), (adv_from, adv_to))):
        for j in range(PIECES):
            part = pl.ds(j * rows, rows)
            moves.append(pltpu.make_async_copy(source.at[part], target.at[part], sems.at[i, j]))
    for move in moves:
        move.start()
    for move in moves:
        move.wait()


def on_device(queries, keys, values, state, timestep, gate_table):
    width = HEADS * HEAD_DIM
    anywhere = pl.BlockSpec(memory_space=pltpu.HBM)
    block = jax.ShapeDtypeStruct((TOK, width), jnp.bfloat16)
    heads = (HEADS, TOK, HEAD_DIM)
    velocity, advanced = pl.pallas_call(
        kernel,
        out_shape=(block, block),
        in_specs=[
            pl.BlockSpec(memory_space=pltpu.SMEM),
            anywhere, anywhere, anywhere, anywhere, anywhere,
        ],
        out_specs=(anywhere, anywhere),
        scratch_shapes=[
            pltpu.VMEM((5, 2 * HEADS, TOK, HEAD_DIM), jnp.bfloat16),
            pltpu.VMEM((KEPT, TOK, 1), jnp.float32),
            pltpu.VMEM((KEPT, TOK, 1), jnp.float32),
            pltpu.VMEM((KEPT, TOK, HEAD_DIM), jnp.float32),
            pltpu.VMEM(heads, jnp.bfloat16),
            pltpu.VMEM(heads, jnp.bfloat16),
            pltpu.VMEM(heads, jnp.bfloat16),
            pltpu.VMEM(heads, jnp.bfloat16),
            pltpu.VMEM((STEPS, width), jnp.bfloat16),
            pltpu.VMEM((HEADS, 8, HEAD_DIM), jnp.float32),
            pltpu.VMEM((2, TOK, HEAD_DIM), jnp.bfloat16),
        ]
        + [pltpu.SemaphoreType.DMA((2 * HEADS,))] * 9
        + [pltpu.SemaphoreType.DMA((HEADS,))] * 5
        + [pltpu.SemaphoreType.DMA]
        + [pltpu.SemaphoreType.DMA((2,))] * 2
        + [pltpu.SemaphoreType.REGULAR] * 2,
        compiler_params=pltpu.CompilerParams(
            collective_id=0, has_side_effects=True, vmem_limit_bytes=32 << 20
        ),
        name="window_attention",
    )(timestep, *[pltpu.with_memory_space_constraint(a, pltpu.HBM) for a in (gate_table, queries[0], keys[0], values[0], state[0])])
    velocity, advanced = pl.pallas_call(
        write_out,
        out_shape=(block, block),
        in_specs=[pl.BlockSpec(memory_space=pltpu.VMEM)] * 2,
        out_specs=(anywhere, anywhere),
        scratch_shapes=[pltpu.SemaphoreType.DMA((2, PIECES))],
        compiler_params=pltpu.CompilerParams(vmem_limit_bytes=16 << 20),
        name="write_out",
    )(velocity, advanced)
    return (velocity[None], advanced[None])


def solution(mesh):
    placed = (
        P("level", "seq", None),
        P("level", "seq", None),
        P("level", "seq", None),
        P("level", "seq", None),
        P("level"),
        P(),
    )
    return jax.shard_map(
        on_device,
        mesh=mesh,
        in_specs=placed,
        out_specs=(P("level", "seq", None), P("level", "seq", None)),
        check_vma=False,
    )
```

```python
import math

import jax
import jax.numpy as jnp
from jax import lax
from jax.experimental import pallas as pl
from jax.experimental.pallas import tpu as pltpu
from jax.sharding import PartitionSpec as P

HEADS = 12
HEAD_DIM = 128
STEPS = 16
TOK = 256
N_LEVEL = 16
N_Y = 8
N_Z = 8
WINDOW = 3
PIECES = 2
LAG_PASS = 2
LAG_COMPUTE = 2
LAG_RELAY = 3
ROWS = (5, 6, 0, 1, 2, 3, 0)
SLOTS = (0, 0, 0, 0, 0, 0, 1)
RELAYED = len(ROWS)
KEPT = 4
MESH = pl.DeviceIdType.MESH
OWN, SIB, ACROSS, ALONG, SHARED = range(5)
FLOOR_VALUE = -1e30


def columns(ref, head):
    return ref.at[:, pl.ds(pl.multiple_of(head * HEAD_DIM, HEAD_DIM), HEAD_DIM)]


def kernel(
    ts_ref, gate_hbm, q_hbm, k_hbm, v_hbm, s_hbm, vel_hbm, adv_hbm,
    kv, tops, totals, sums, qs, ss, upd, vel, gate_table, gates, relay,
    sem_own, send_sib, recv_sib, send_x, recv_x, send_z, recv_z, send_d, recv_d,
    sem_q, sem_s, sem_vel, send_l, recv_l, sem_gate, send_r, recv_r, along_ready, level_ready,
):
    level = lax.axis_index("level")
    seq = lax.axis_index("seq")
    core = seq % 2
    x_hi = (seq // 2) % 2
    z = seq // 4
    x_lo = level // N_Y
    y = level % N_Y

    def at(z_, x_hi_, core_):
        return (level, z_ * 4 + x_hi_ * 2 + core_)

    def on_level(x_lo_, y_):
        return (x_lo_ * N_Y + y_, seq)

    sibling = at(z, x_hi, 1 - core)
    across = at(z, 1 - x_hi, core)
    along_to = at((z + 1 + (N_Z - 2) * x_hi) % N_Z, x_hi, core)
    level_to = ((level + N_LEVEL - 1) % N_LEVEL, seq)
    end = ((z == 0) & (x_hi == 0)) | ((z == N_Z - 1) & (x_hi == 1))
    passes = jnp.logical_not(((z == 0) & (x_hi == 1)) | ((z == N_Z - 1) & (x_hi == 0)))
    shares_across = core == x_hi

    barrier = pltpu.get_barrier_semaphore()

    def greet(device):
        pl.semaphore_signal(barrier, inc=1, device_id=device, device_id_type=MESH)

    greet(across)
    greet(sibling)

    @pl.when(z < N_Z - 1)
    def _():
        greet(at(z + 1, x_hi, core))

    @pl.when(y < N_Y - 1)
    def _():
        greet(on_level(x_lo, y + 1))

    @pl.when(y == 0)
    def _():
        for row in range(N_Y):
            greet(on_level(1 - x_lo, row))

    def load_gate():
        return pltpu.make_async_copy(gate_hbm, gate_table, sem_gate)

    def own_part(h, kind):
        return columns(v_hbm if kind else k_hbm, h)

    def load_own(h, kind):
        u = 2 * h + kind
        return pltpu.make_async_copy(own_part(h, kind), kv.at[OWN, u], sem_own.at[u])

    def load_q(h):
        return pltpu.make_async_copy(columns(q_hbm, h), qs.at[h], sem_q.at[h])

    def load_s(h):
        return pltpu.make_async_copy(columns(s_hbm, h), ss.at[h], sem_s.at[h])

    def store_vel(h):
        return pltpu.make_async_copy(vel.at[h], columns(vel_hbm, h), sem_vel)

    def remote(source, target, send, recv, device):
        return pltpu.make_async_remote_copy(
            source, target, send, recv, device_id=device, device_id_type=MESH
        )

    def to_sibling(h):
        both = pl.ds(2 * h, 2)
        return remote(
            kv.at[OWN, both], kv.at[SIB, both], send_sib, recv_sib.at[h], sibling
        )

    def to_across(h, kind):
        u = 2 * h + kind
        return remote(kv.at[OWN, u], kv.at[ACROSS, u], send_x, recv_x.at[u], across)

    def to_along(u):
        return remote(kv.at[ACROSS, u], kv.at[ALONG, u], send_z, recv_z.at[u], along_to)

    def own_as_along(u):
        return pltpu.make_async_copy(kv.at[OWN, u], kv.at[ALONG, u], recv_z.at[u])

    def share(slot, u):
        return remote(kv.at[slot, u], kv.at[SHARED, u], send_d, recv_d.at[u], sibling)

    def to_level(h):
        return remote(upd.at[h], columns(adv_hbm, h), send_l, recv_l, level_to)

    def to_relay(h):
        return remote(
            upd.at[h], relay.at[SLOTS[h]], send_l, recv_r.at[SLOTS[h]],
            on_level(1 - x_lo, ROWS[h]),
        )

    def from_relay(h):
        return remote(
            relay.at[SLOTS[h]], columns(adv_hbm, h), send_r.at[SLOTS[h]], recv_l,
            on_level(x_lo, N_Y - 1),
        )

    def send_own(h):
        for kind in range(2):
            load_own(h, kind).wait()
        for kind in range(2):
            to_across(h, kind).start()
        to_sibling(h).start()

    def load_rest(h):
        load_q(h).start()
        load_s(h).start()

    for h in range(HEADS):
        for kind in range(2):
            load_own(h, kind).start()
    load_gate().start()
    pl.semaphore_wait(barrier, 3 + (z > 0).astype(jnp.int32) + (y > 0).astype(jnp.int32))
    for h in range(WINDOW):
        send_own(h)
    @pl.when((x_hi == 0) & (z > 0))
    def _():
        pl.semaphore_signal(
            along_ready, inc=1, device_id=at(z - 1, x_hi, core), device_id_type=MESH
        )

    pl.semaphore_signal(
        level_ready, inc=1, device_id=on_level(1 - x_lo, 0), device_id_type=MESH
    )
    for h in range(HEADS):
        load_rest(h)

    load_gate().wait()
    step_index = ts_ref[0]
    chosen = lax.broadcasted_iota(jnp.int32, (STEPS, HEADS * HEAD_DIM), 0) == step_index - 1
    gate_row = jnp.sum(
        jnp.where(chosen, gate_table[...].astype(jnp.float32), 0.0), axis=0, keepdims=True
    )
    for h in range(HEADS):
        gates[h] = jnp.broadcast_to(gate_row[:, h * HEAD_DIM : (h + 1) * HEAD_DIM], (8, HEAD_DIM))
    factor = -(2.0 * step_index.astype(jnp.float32) - 1.0) / (STEPS * STEPS)

    bias_along = jnp.where(end, FLOOR_VALUE, 0.0)
    bias_shared = jnp.where(end & shares_across, FLOOR_VALUE, 0.0)
    scaling = math.log2(math.e) / math.sqrt(HEAD_DIM)

    def score(h, slot):
        part = (
            lax.dot_general(
                qs[h], kv[slot, 2 * h], (((1,), (1,)), ((), ())),
                preferred_element_type=jnp.float32,
            )
            * scaling
        )
        if slot == ALONG:
            part = part + bias_along
        if slot == SHARED:
            part = part + bias_shared
        return part

    def weigh(h, slots, scores, top):
        total = None
        blended = None
        for slot, part in zip(slots, scores):
            weights = jnp.exp2(part - top)
            total = weights if total is None else total + weights
            product = jnp.dot(
                weights.astype(jnp.bfloat16), kv[slot, 2 * h + 1],
                preferred_element_type=jnp.float32,
            )
            blended = product if blended is None else blended + product
        return jnp.sum(total, axis=-1, keepdims=True), blended

    def highest(scores):
        top = scores[0]
        for part in scores[1:]:
            top = jnp.maximum(top, part)
        return jnp.max(top, axis=-1, keepdims=True)

    FIRST, REST = (OWN, SIB, ACROSS), (ALONG, SHARED)

    def compute_first(h):
        place = lax.rem(h, KEPT)
        scores = [score(h, slot) for slot in FIRST]
        top = highest(scores)
        total, blended = weigh(h, FIRST, scores, top)
        tops[place] = top
        totals[place] = total
        sums[place] = blended

    def compute_rest(h):
        place = lax.rem(h, KEPT)
        scores = [score(h, slot) for slot in REST]
        top = jnp.maximum(highest(scores), tops[place])
        total, blended = weigh(h, REST, scores, top)
        kept = jnp.exp2(tops[place] - top)
        total = total + totals[place] * kept
        attended = (blended + sums[place] * kept) / total
        velocity = (gates[h][0:1] * attended).astype(jnp.bfloat16)
        vel[h] = velocity
        upd[h] = (ss[h].astype(jnp.float32) + factor * velocity.astype(jnp.float32)).astype(
            jnp.bfloat16
        )

    def step(t, carry):
        def arrived(kind):
            u = 2 * t + kind
            to_across(t, kind).wait_recv()

            @pl.when(passes)
            def _():
                to_along(u).start()

            @pl.when(shares_across)
            def _():
                share(ACROSS, u).start()

        @pl.when(t < HEADS)
        def _():
            arrived(0)

        @pl.when((t >= LAG_PASS) & (t < HEADS + LAG_PASS))
        def _():
            for kind in range(2):
                u = 2 * (t - LAG_PASS) + kind

                @pl.when(end)
                def _():
                    own_as_along(u).start()

                to_along(u).wait_recv()

                @pl.when(jnp.logical_not(shares_across))
                def _():
                    share(ALONG, u).start()

        @pl.when(t < HEADS)
        def _():
            arrived(1)

        @pl.when(t + WINDOW < HEADS)
        def _():
            send_own(t + WINDOW)

        @pl.when(t >= LAG_COMPUTE)
        def _():
            h = t - LAG_COMPUTE
            for kind in range(2):
                share(ACROSS, 2 * h + kind).wait_recv()
            load_s(h).wait()
            compute_rest(h)

            @pl.when((y == 0) & (h == 0))
            def _():
                pl.semaphore_wait(level_ready, N_Y)

            for i in range(RELAYED):

                @pl.when((y == 0) & (h == i))
                def _():
                    to_relay(i).start()

            @pl.when((y > 0) | (h >= RELAYED))
            def _():
                to_level(h).start()

            store_vel(h).start()

        @pl.when(t < HEADS)
        def _():
            to_sibling(t).wait_recv()
            load_q(t).wait()
            compute_first(t)

        for i in range(RELAYED):

            @pl.when((y == ROWS[i]) & (t == i + LAG_COMPUTE + LAG_RELAY))
            def _():
                to_relay(i).wait_recv()
                from_relay(i).start()

        return carry

    @pl.when((x_hi == 0) & (z < N_Z - 1))
    def _():
        pl.semaphore_wait(along_ready, 1)

    lax.fori_loop(0, HEADS + LAG_COMPUTE, step, 0)

    remote(kv.at[OWN], kv.at[SIB], send_sib, recv_sib.at[0], sibling).wait_send()
    remote(kv.at[OWN], kv.at[ACROSS], send_x, recv_x.at[0], across).wait_send()
    remote(kv.at[ACROSS], kv.at[SHARED], send_d, recv_d.at[0], sibling).wait_send()
    remote(upd, upd, send_l, recv_l, level_to).wait_send()

    @pl.when(passes)
    def _():
        remote(kv.at[ACROSS], kv.at[ALONG], send_z, recv_z.at[0], along_to).wait_send()

    pltpu.make_async_copy(vel_hbm, vel_hbm, sem_vel).wait()
    remote(adv_hbm, adv_hbm, send_l, recv_l, level_to).wait_recv()

    for i in range(RELAYED):

        @pl.when(y == ROWS[i])
        def _():
            from_relay(i).wait_send()


def write_out(vel_from, adv_from, vel_to, adv_to, sems):
    rows = TOK // PIECES
    moves = []
    for i, (source, target) in enumerate(((vel_from, vel_to), (adv_from, adv_to))):
        for j in range(PIECES):
            part = pl.ds(j * rows, rows)
            moves.append(pltpu.make_async_copy(source.at[part], target.at[part], sems.at[i, j]))
    for move in moves:
        move.start()
    for move in moves:
        move.wait()


def on_device(queries, keys, values, state, timestep, gate_table):
    width = HEADS * HEAD_DIM
    anywhere = pl.BlockSpec(memory_space=pltpu.HBM)
    block = jax.ShapeDtypeStruct((TOK, width), jnp.bfloat16)
    heads = (HEADS, TOK, HEAD_DIM)
    velocity, advanced = pl.pallas_call(
        kernel,
        out_shape=(block, block),
        in_specs=[
            pl.BlockSpec(memory_space=pltpu.SMEM),
            anywhere, anywhere, anywhere, anywhere, anywhere,
        ],
        out_specs=(anywhere, anywhere),
        scratch_shapes=[
            pltpu.VMEM((5, 2 * HEADS, TOK, HEAD_DIM), jnp.bfloat16),
            pltpu.VMEM((KEPT, TOK, 1), jnp.float32),
            pltpu.VMEM((KEPT, TOK, 1), jnp.float32),
            pltpu.VMEM((KEPT, TOK, HEAD_DIM), jnp.float32),
            pltpu.VMEM(heads, jnp.bfloat16),
            pltpu.VMEM(heads, jnp.bfloat16),
            pltpu.VMEM(heads, jnp.bfloat16),
            pltpu.VMEM(heads, jnp.bfloat16),
            pltpu.VMEM((STEPS, width), jnp.bfloat16),
            pltpu.VMEM((HEADS, 8, HEAD_DIM), jnp.float32),
            pltpu.VMEM((2, TOK, HEAD_DIM), jnp.bfloat16),
        ]
        + [pltpu.SemaphoreType.DMA((2 * HEADS,))]
        + [pltpu.SemaphoreType.DMA, pltpu.SemaphoreType.DMA((2 * HEADS,))] * 4
        + [pltpu.SemaphoreType.DMA((HEADS,))] * 2
        + [pltpu.SemaphoreType.DMA] * 3
        + [pltpu.SemaphoreType.DMA]
        + [pltpu.SemaphoreType.DMA((2,))] * 2
        + [pltpu.SemaphoreType.REGULAR] * 2,
        compiler_params=pltpu.CompilerParams(
            collective_id=0, has_side_effects=True, vmem_limit_bytes=32 << 20
        ),
        name="window_attention",
    )(timestep, *[pltpu.with_memory_space_constraint(a, pltpu.HBM) for a in (gate_table, queries[0], keys[0], values[0], state[0])])
    velocity, advanced = pl.pallas_call(
        write_out,
        out_shape=(block, block),
        in_specs=[pl.BlockSpec(memory_space=pltpu.VMEM)] * 2,
        out_specs=(anywhere, anywhere),
        scratch_shapes=[pltpu.SemaphoreType.DMA((2, PIECES))],
        compiler_params=pltpu.CompilerParams(vmem_limit_bytes=16 << 20),
        name="write_out",
    )(velocity, advanced)
    return (velocity[None], advanced[None])


def solution(mesh):
    placed = (
        P("level", "seq", None),
        P("level", "seq", None),
        P("level", "seq", None),
        P("level", "seq", None),
        P("level"),
        P(),
    )
    return jax.shard_map(
        on_device,
        mesh=mesh,
        in_specs=placed,
        out_specs=(P("level", "seq", None), P("level", "seq", None)),
        check_vma=False,
    )
```

```python
import math

import jax
import jax.numpy as jnp
from jax import lax
from jax.experimental import pallas as pl
from jax.experimental.pallas import tpu as pltpu
from jax.sharding import PartitionSpec as P

HEADS = 12
HEAD_DIM = 128
STEPS = 16
TOK = 256
N_LEVEL = 16
N_Y = 8
N_Z = 8
WINDOW = 3
PIECES = 2
LAG_PASS = 2
LAG_COMPUTE = 2
LAG_RELAY = 3
ROWS = (5, 6, 0, 1, 2, 3, 0)
SLOTS = (0, 0, 0, 0, 0, 0, 1)
RELAYED = len(ROWS)
KEPT = 4
MESH = pl.DeviceIdType.MESH
OWN, SIB, ACROSS, ALONG, SHARED = range(5)
FLOOR_VALUE = -1e30


def columns(ref, head):
    return ref.at[:, pl.ds(pl.multiple_of(head * HEAD_DIM, HEAD_DIM), HEAD_DIM)]


def kernel(
    ts_ref, gate_hbm, q_hbm, k_hbm, v_hbm, s_hbm, vel_hbm, adv_hbm,
    kv, tops, totals, sums, qs, ss, upd, vel, gate_table, gates, relay,
    sem_own, send_sib, recv_sib, send_x, recv_x, send_z, recv_z, send_d, recv_d,
    sem_q, sem_s, sem_vel, send_l, recv_l, sem_gate, send_r, recv_r, along_ready, level_ready,
):
    level = lax.axis_index("level")
    seq = lax.axis_index("seq")
    core = seq % 2
    x_hi = (seq // 2) % 2
    z = seq // 4
    x_lo = level // N_Y
    y = level % N_Y

    def at(z_, x_hi_, core_):
        return (level, z_ * 4 + x_hi_ * 2 + core_)

    def on_level(x_lo_, y_):
        return (x_lo_ * N_Y + y_, seq)

    sibling = at(z, x_hi, 1 - core)
    across = at(z, 1 - x_hi, core)
    along_to = at((z + 1 + (N_Z - 2) * x_hi) % N_Z, x_hi, core)
    level_to = ((level + N_LEVEL - 1) % N_LEVEL, seq)
    end = ((z == 0) & (x_hi == 0)) | ((z == N_Z - 1) & (x_hi == 1))
    passes = jnp.logical_not(((z == 0) & (x_hi == 1)) | ((z == N_Z - 1) & (x_hi == 0)))
    shares_across = core == x_hi

    barrier = pltpu.get_barrier_semaphore()

    def greet(device):
        pl.semaphore_signal(barrier, inc=1, device_id=device, device_id_type=MESH)

    greet(across)
    greet(sibling)

    @pl.when(z < N_Z - 1)
    def _():
        greet(at(z + 1, x_hi, core))

    @pl.when(y < N_Y - 1)
    def _():
        greet(on_level(x_lo, y + 1))

    @pl.when(y == 0)
    def _():
        for row in range(N_Y):
            greet(on_level(1 - x_lo, row))

    def load_gate():
        return pltpu.make_async_copy(gate_hbm, gate_table, sem_gate)

    def own_part(h, kind):
        return columns(v_hbm if kind else k_hbm, h)

    def load_own(h, kind):
        u = 2 * h + kind
        return pltpu.make_async_copy(own_part(h, kind), kv.at[OWN, u], sem_own.at[u])

    def load_q(h):
        return pltpu.make_async_copy(columns(q_hbm, h), qs.at[h], sem_q.at[h])

    def load_s(h):
        return pltpu.make_async_copy(columns(s_hbm, h), ss.at[h], sem_s.at[h])

    def store_vel(h):
        return pltpu.make_async_copy(vel.at[h], columns(vel_hbm, h), sem_vel)

    def remote(source, target, send, recv, device):
        return pltpu.make_async_remote_copy(
            source, target, send, recv, device_id=device, device_id_type=MESH
        )

    def to_sibling(h):
        both = pl.ds(2 * h, 2)
        return remote(
            kv.at[OWN, both], kv.at[SIB, both], send_sib, recv_sib.at[h], sibling
        )

    def to_across(h, kind):
        u = 2 * h + kind
        return remote(kv.at[OWN, u], kv.at[ACROSS, u], send_x, recv_x.at[u], across)

    def to_along(u):
        return remote(kv.at[ACROSS, u], kv.at[ALONG, u], send_z, recv_z.at[u], along_to)

    def own_as_along(u):
        return pltpu.make_async_copy(kv.at[OWN, u], kv.at[ALONG, u], recv_z.at[u])

    def share(slot, u):
        return remote(kv.at[slot, u], kv.at[SHARED, u], send_d, recv_d.at[u], sibling)

    def to_level(h):
        return remote(upd.at[h], columns(adv_hbm, h), send_l, recv_l, level_to)

    def part_to_level(h, rows):
        return remote(
            upd.at[h, rows], columns(adv_hbm.at[rows], h), send_l, recv_l, level_to
        )

    def to_relay(h):
        return remote(
            upd.at[h], relay.at[SLOTS[h]], send_l, recv_r.at[SLOTS[h]],
            on_level(1 - x_lo, ROWS[h]),
        )

    def from_relay(h):
        return remote(
            relay.at[SLOTS[h]], columns(adv_hbm, h), send_r.at[SLOTS[h]], recv_l,
            on_level(x_lo, N_Y - 1),
        )

    def send_own(h):
        for kind in range(2):
            load_own(h, kind).wait()
        for kind in range(2):
            to_across(h, kind).start()
        to_sibling(h).start()

    def load_rest(h):
        load_q(h).start()
        load_s(h).start()

    for h in range(HEADS):
        for kind in range(2):
            load_own(h, kind).start()
    load_gate().start()
    pl.semaphore_wait(barrier, 3 + (z > 0).astype(jnp.int32) + (y > 0).astype(jnp.int32))
    for h in range(WINDOW):
        send_own(h)
    @pl.when((x_hi == 0) & (z > 0))
    def _():
        pl.semaphore_signal(
            along_ready, inc=1, device_id=at(z - 1, x_hi, core), device_id_type=MESH
        )

    pl.semaphore_signal(
        level_ready, inc=1, device_id=on_level(1 - x_lo, 0), device_id_type=MESH
    )
    for h in range(HEADS):
        load_rest(h)

    load_gate().wait()
    step_index = ts_ref[0]
    chosen = lax.broadcasted_iota(jnp.int32, (STEPS, HEADS * HEAD_DIM), 0) == step_index - 1
    gate_row = jnp.sum(
        jnp.where(chosen, gate_table[...].astype(jnp.float32), 0.0), axis=0, keepdims=True
    )
    for h in range(HEADS):
        gates[h] = jnp.broadcast_to(gate_row[:, h * HEAD_DIM : (h + 1) * HEAD_DIM], (8, HEAD_DIM))
    factor = -(2.0 * step_index.astype(jnp.float32) - 1.0) / (STEPS * STEPS)

    bias_along = jnp.where(end, FLOOR_VALUE, 0.0)
    bias_shared = jnp.where(end & shares_across, FLOOR_VALUE, 0.0)
    scaling = math.log2(math.e) / math.sqrt(HEAD_DIM)

    def score(h, slot, rows):
        part = (
            lax.dot_general(
                qs[h, rows], kv[slot, 2 * h], (((1,), (1,)), ((), ())),
                preferred_element_type=jnp.float32,
            )
            * scaling
        )
        if slot == ALONG:
            part = part + bias_along
        if slot == SHARED:
            part = part + bias_shared
        return part

    def weigh(h, slots, scores, top):
        total = None
        blended = None
        for slot, part in zip(slots, scores):
            weights = jnp.exp2(part - top)
            total = weights if total is None else total + weights
            product = jnp.dot(
                weights.astype(jnp.bfloat16), kv[slot, 2 * h + 1],
                preferred_element_type=jnp.float32,
            )
            blended = product if blended is None else blended + product
        return jnp.sum(total, axis=-1, keepdims=True), blended

    def highest(scores):
        top = scores[0]
        for part in scores[1:]:
            top = jnp.maximum(top, part)
        return jnp.max(top, axis=-1, keepdims=True)

    FIRST, REST = (OWN, SIB, ACROSS), (ALONG, SHARED)

    def compute_first(h):
        place = lax.rem(h, KEPT)
        scores = [score(h, slot, pl.ds(0, TOK)) for slot in FIRST]
        top = highest(scores)
        total, blended = weigh(h, FIRST, scores, top)
        tops[place] = top
        totals[place] = total
        sums[place] = blended

    def compute_rest(h, rows):
        place = lax.rem(h, KEPT)
        scores = [score(h, slot, rows) for slot in REST]
        earlier = tops[place, rows]
        top = jnp.maximum(highest(scores), earlier)
        total, blended = weigh(h, REST, scores, top)
        kept = jnp.exp2(earlier - top)
        total = total + totals[place, rows] * kept
        attended = (blended + sums[place, rows] * kept) / total
        velocity = (gates[h][0:1] * attended).astype(jnp.bfloat16)
        vel[h, rows] = velocity
        upd[h, rows] = (
            ss[h, rows].astype(jnp.float32) + factor * velocity.astype(jnp.float32)
        ).astype(jnp.bfloat16)

    def step(t, carry):
        def arrived(kind):
            u = 2 * t + kind
            to_across(t, kind).wait_recv()

            @pl.when(passes)
            def _():
                to_along(u).start()

            @pl.when(shares_across)
            def _():
                share(ACROSS, u).start()

        @pl.when(t < HEADS)
        def _():
            arrived(0)

        @pl.when((t >= LAG_PASS) & (t < HEADS + LAG_PASS))
        def _():
            for kind in range(2):
                u = 2 * (t - LAG_PASS) + kind

                @pl.when(end)
                def _():
                    own_as_along(u).start()

                to_along(u).wait_recv()

                @pl.when(jnp.logical_not(shares_across))
                def _():
                    share(ALONG, u).start()

        @pl.when(t < HEADS)
        def _():
            arrived(1)

        @pl.when(t + WINDOW < HEADS)
        def _():
            send_own(t + WINDOW)

        @pl.when(t >= LAG_COMPUTE)
        def _():
            h = t - LAG_COMPUTE
            for kind in range(2):
                share(ACROSS, 2 * h + kind).wait_recv()
            load_s(h).wait()

            @pl.when(h < HEADS - 1)
            def _():
                compute_rest(h, pl.ds(0, TOK))

            @pl.when(h == HEADS - 1)
            def _():
                for half in range(2):
                    rows = pl.ds(half * (TOK // 2), TOK // 2)
                    compute_rest(h, rows)
                    part_to_level(h, rows).start()

            @pl.when((y == 0) & (h == 0))
            def _():
                pl.semaphore_wait(level_ready, N_Y)

            for i in range(RELAYED):

                @pl.when((y == 0) & (h == i))
                def _():
                    to_relay(i).start()

            @pl.when(((y > 0) | (h >= RELAYED)) & (h < HEADS - 1))
            def _():
                to_level(h).start()

            store_vel(h).start()

        @pl.when(t < HEADS)
        def _():
            to_sibling(t).wait_recv()
            load_q(t).wait()
            compute_first(t)

        for i in range(RELAYED):

            @pl.when((y == ROWS[i]) & (t == i + LAG_COMPUTE + LAG_RELAY))
            def _():
                to_relay(i).wait_recv()
                from_relay(i).start()

        return carry

    @pl.when((x_hi == 0) & (z < N_Z - 1))
    def _():
        pl.semaphore_wait(along_ready, 1)

    lax.fori_loop(0, HEADS + LAG_COMPUTE, step, 0)

    remote(kv.at[OWN], kv.at[SIB], send_sib, recv_sib.at[0], sibling).wait_send()
    remote(kv.at[OWN], kv.at[ACROSS], send_x, recv_x.at[0], across).wait_send()
    remote(kv.at[ACROSS], kv.at[SHARED], send_d, recv_d.at[0], sibling).wait_send()
    remote(upd, upd, send_l, recv_l, level_to).wait_send()

    @pl.when(passes)
    def _():
        remote(kv.at[ACROSS], kv.at[ALONG], send_z, recv_z.at[0], along_to).wait_send()

    pltpu.make_async_copy(vel_hbm, vel_hbm, sem_vel).wait()
    remote(adv_hbm, adv_hbm, send_l, recv_l, level_to).wait_recv()

    for i in range(RELAYED):

        @pl.when(y == ROWS[i])
        def _():
            from_relay(i).wait_send()


def write_out(vel_from, adv_from, vel_to, adv_to, sems):
    rows = TOK // PIECES
    moves = []
    for i, (source, target) in enumerate(((vel_from, vel_to), (adv_from, adv_to))):
        for j in range(PIECES):
            part = pl.ds(j * rows, rows)
            moves.append(pltpu.make_async_copy(source.at[part], target.at[part], sems.at[i, j]))
    for move in moves:
        move.start()
    for move in moves:
        move.wait()


def on_device(queries, keys, values, state, timestep, gate_table):
    width = HEADS * HEAD_DIM
    anywhere = pl.BlockSpec(memory_space=pltpu.HBM)
    block = jax.ShapeDtypeStruct((TOK, width), jnp.bfloat16)
    heads = (HEADS, TOK, HEAD_DIM)
    velocity, advanced = pl.pallas_call(
        kernel,
        out_shape=(block, block),
        in_specs=[
            pl.BlockSpec(memory_space=pltpu.SMEM),
            anywhere, anywhere, anywhere, anywhere, anywhere,
        ],
        out_specs=(anywhere, anywhere),
        scratch_shapes=[
            pltpu.VMEM((5, 2 * HEADS, TOK, HEAD_DIM), jnp.bfloat16),
            pltpu.VMEM((KEPT, TOK, 1), jnp.float32),
            pltpu.VMEM((KEPT, TOK, 1), jnp.float32),
            pltpu.VMEM((KEPT, TOK, HEAD_DIM), jnp.float32),
            pltpu.VMEM(heads, jnp.bfloat16),
            pltpu.VMEM(heads, jnp.bfloat16),
            pltpu.VMEM(heads, jnp.bfloat16),
            pltpu.VMEM(heads, jnp.bfloat16),
            pltpu.VMEM((STEPS, width), jnp.bfloat16),
            pltpu.VMEM((HEADS, 8, HEAD_DIM), jnp.float32),
            pltpu.VMEM((2, TOK, HEAD_DIM), jnp.bfloat16),
        ]
        + [pltpu.SemaphoreType.DMA((2 * HEADS,))]
        + [pltpu.SemaphoreType.DMA, pltpu.SemaphoreType.DMA((2 * HEADS,))] * 4
        + [pltpu.SemaphoreType.DMA((HEADS,))] * 2
        + [pltpu.SemaphoreType.DMA] * 3
        + [pltpu.SemaphoreType.DMA]
        + [pltpu.SemaphoreType.DMA((2,))] * 2
        + [pltpu.SemaphoreType.REGULAR] * 2,
        compiler_params=pltpu.CompilerParams(
            collective_id=0, has_side_effects=True, vmem_limit_bytes=32 << 20
        ),
        name="window_attention",
    )(timestep, *[pltpu.with_memory_space_constraint(a, pltpu.HBM) for a in (gate_table, queries[0], keys[0], values[0], state[0])])
    velocity, advanced = pl.pallas_call(
        write_out,
        out_shape=(block, block),
        in_specs=[pl.BlockSpec(memory_space=pltpu.VMEM)] * 2,
        out_specs=(anywhere, anywhere),
        scratch_shapes=[pltpu.SemaphoreType.DMA((2, PIECES))],
        compiler_params=pltpu.CompilerParams(vmem_limit_bytes=16 << 20),
        name="write_out",
    )(velocity, advanced)
    return (velocity[None], advanced[None])


def solution(mesh):
    placed = (
        P("level", "seq", None),
        P("level", "seq", None),
        P("level", "seq", None),
        P("level", "seq", None),
        P("level"),
        P(),
    )
    return jax.shard_map(
        on_device,
        mesh=mesh,
        in_specs=placed,
        out_specs=(P("level", "seq", None), P("level", "seq", None)),
        check_vma=False,
    )
```
